32 devices in a mesh: dp: 4 (over x, core), expert: 8 (over z, y).
Axes of the slice: x: 2, y: 2, z: 4, core: 2. Of those that a mesh axis runs over, the one named last changes fastest.
Arguments:
- tokens_in: bfloat16 [2, 256, 2048], P(None, 'expert', 'dp'), may hold values from -6 to 6
- route_ids: int32 [2, 256, 8], P(None, 'expert'), may hold values from 0 to 15, all different within a row; in each aligned block of 32 rows (0 to 31, 32 to 63, ..., all dimensions but the last counted through in order) at most 32 rows name the same one
- route_gates: float32 [2, 256, 8], P(None, 'expert'), may hold values from 0.1 to 1
- cotangent: bfloat16 [2, 256, 2048], P(None, 'expert', 'dp'), may hold values from -0.75 to 0.75
- gate_proj: bfloat16 [16, 1024, 1536], P(None, 'expert', 'dp'), may hold values from -0.125 to 0.125
- up_proj: bfloat16 [16, 1024, 1536], P(None, 'expert', 'dp'), may hold values from -0.125 to 0.125
- down_proj: bfloat16 [16, 1024, 1536], P(None, 'expert', 'dp'), may hold values from -0.21875 to 0.21875
- replica_plan: int32 [2, 8], replicated, may hold values from 0 to 15, as said below
- capacity: int32 [2, 16], replicated, may hold values from 8 to 16, as said below
Outputs:
- y_out: bfloat16 [2, 256, 2048], P(None, 'expert', 'dp')
- x_grad: bfloat16 [2, 256, 2048], P(None, 'expert', 'dp')
- gate_grad: bfloat16 [16, 1024, 1536], P(None, 'expert', 'dp')
- up_grad: bfloat16 [16, 1024, 1536], P(None, 'expert', 'dp')
- down_grad: bfloat16 [16, 1024, 1536], P(None, 'expert', 'dp')
The draws below stay inside these ranges and needn't reach their ends.
Inputs may be any that keep to these rules, and one draw needn't show every extreme that they name: `route_ids`: each token names 8 different experts; among the tokens of one micro-batch on one index of the expert axis (an aligned block of 32), no expert is named more than 2 * 16 times. `replica_plan`: an expert may fill the replica slot of several devices, or of none. Some expert has capacity 16 in every micro-batch.
All inputs are finite; a program needn't handle non-finite values.
Results may differ from the reference program's by a relative error of at most 0.012.
Values may be sent and summed in bfloat16 or wider, within the bound.
A program may use at most 192 MiB of HBM per device.

```python
import math
import jax
import jax.numpy as jnp
import numpy as np
from jax import lax

D = 2048
FF = 768
TOPK = 8
MICRO = 2
TOK_DEV = 32
EXPERTS = 16
CAP = 16
TOKENS = 256
N_DP = 4
N_EXPERT = 8


def draw_replica_plan(key, part):
    subkeys = jax.random.split(key, 2 * MICRO)
    per_batch = []
    for batch_index in range(MICRO):
        shuffled = jax.random.permutation(subkeys[2 * batch_index], EXPERTS)
        chosen = jax.random.randint(subkeys[2 * batch_index + 1], (EXPERTS // 2,), 0, 8)
        per_batch.append(shuffled[chosen])
    return jnp.stack(per_batch).astype(jnp.int32)


def draw_capacity(key, part):
    first_key, second_key = jax.random.split(key)
    drawn = jax.random.randint(first_key, (MICRO, EXPERTS), max(1, CAP // 2), CAP + 1)
    forced = jax.random.randint(second_key, (MICRO, 1), 0, EXPERTS)
    return jnp.where(jnp.arange(EXPERTS)[None, :] == forced, CAP, drawn).astype(jnp.int32)


def block_levels(own_key, extent, pieces, low, top_value):
    loudness = 1.0
    for position, blocks in pieces:
        steps = jax.random.uniform(jax.random.fold_in(jax.random.fold_in(own_key, 6), position), (blocks,), jnp.float32, low / len(pieces), top_value / len(pieces))
        loudness = loudness * jnp.repeat(jnp.exp(steps), extent[position] // blocks).reshape((-1,) + (1,) * (len(extent) - 1 - position))
    return loudness


def assign_block(key, own, number, rows, amount, top, reach, slope):
    order = jax.random.permutation(key, amount)
    crowded, ordinary = portions_of(amount, rows * top, reach, slope, True), portions_of(amount, rows * top, reach, slope, False)
    places = jnp.arange(amount)

    def named(lengths, rotation):
        used = int((lengths > 0).sum())
        fixed = max(1, used // 4)
        moved = fixed + (places - fixed + rotation * (used - fixed)) % max(1, amount - fixed)
        return jnp.zeros((amount,), jnp.int32).at[order[jnp.where(places < fixed, places, moved)]].set(jnp.asarray(lengths, jnp.int32))

    lengths = jnp.where(number % 4 == 0, named(crowded, number // 4), named(ordinary, number - number // 4 - 1))
    mixed = jax.random.permutation(jax.random.fold_in(own, 3), amount)
    giver, taker = mixed[0:amount // 2 * 2:2], mixed[1:amount // 2 * 2:2]
    room = jnp.minimum(lengths[giver] - 1, reach - lengths[taker]) // 2
    room = jnp.where((giver == order[0]) | (taker == order[0]) | (lengths[taker] == 0), 0, jnp.maximum(room, 0))
    moved = jax.random.randint(jax.random.fold_in(own, 4), (amount // 2,), 0, 1 << 20) % (room + 1)
    lengths = lengths.at[giver].add(-moved).at[taker].add(moved)
    labels = jnp.searchsorted(jnp.cumsum(lengths), jnp.arange(rows * top), side="right").astype(jnp.int32)
    grid = labels.reshape(top, rows).T
    grid = grid[jax.random.permutation(jax.random.fold_in(own, 1), rows)]
    rotation = jax.random.randint(jax.random.fold_in(own, 2), (rows, 1), 0, top)
    return jnp.take_along_axis(grid, (jnp.arange(top)[None, :] + rotation) % top, axis=1)


def portions_of(number_of, total, most, skew, full):
    portions = [(1 << 20) // math.isqrt(standing ** skew) + 1 for standing in range(1, number_of + 1)]
    largest = most if full else min(most, max(-(-total // number_of), total * portions[0] // sum(portions)))
    least = 1 if total - largest >= number_of - 1 else 0
    given, spare = [largest] + [least] * (number_of - 1), total - largest - least * (number_of - 1)
    while spare > 0:
        free = [i for i in range(1, number_of) if given[i] < largest] or [i for i in range(1, number_of) if given[i] < most]
        mass, left = sum([portions[i] for i in free]), spare
        for i in free:
            extra = min(most - given[i], max(1, left * portions[i] // mass), spare)
            given[i] = given[i] + extra
            spare = spare - extra
    return np.array(given)


def noise(rng, extent, width, reach, pieces=(), held_as=jnp.bfloat16):
    values = width * jax.random.normal(rng, extent, jnp.float32)
    if pieces:
        values = values * block_levels(rng, extent, pieces, -0.22, 0.18)
    return jnp.clip(values, -reach, reach).astype(held_as)


def setup_inputs(seed: int = 0) -> dict:
    key_list = jax.random.split(jax.random.key(seed), 10)
    tokens_in = noise(key_list[0], (MICRO, TOKENS, D), 1.0, 6.0, ((1, 8), (2, 4)))
    route_ids_keys = jax.random.split(jax.random.fold_in(key_list[1], 1), MICRO * TOKENS // TOK_DEV)
    route_ids_turns = jax.random.permutation(jax.random.fold_in(key_list[1], 3), MICRO * TOKENS // TOK_DEV)
    route_ids = jax.vmap(lambda own, number: assign_block(jax.random.fold_in(key_list[1], 2), own, number, TOK_DEV, EXPERTS, TOPK, 2 * CAP, 2))(route_ids_keys, route_ids_turns).reshape((MICRO, TOKENS, TOPK))
    route_gates = jnp.clip(0.1 + 0.9 * jax.random.uniform(key_list[2], (MICRO, TOKENS, TOPK), jnp.float32) ** block_levels(key_list[2], (MICRO, TOKENS, TOPK), ((1, 8),), -0.2, 0.2), 0.1, 1.0)
    cotangent = noise(key_list[3], (MICRO, TOKENS, D), 0.125, 0.75, ((1, 8), (2, 4)))
    gate_proj = noise(key_list[4], (EXPERTS, D // 2, 2 * FF), D ** -0.5, 0.125, ((1, 8), (2, 4)))
    up_proj = noise(key_list[5], (EXPERTS, D // 2, 2 * FF), D ** -0.5, 0.125, ((1, 8), (2, 4)))
    down_proj = noise(key_list[6], (EXPERTS, D // 2, 2 * FF), FF ** -0.5, 0.21875, ((1, 8), (2, 4)))
    replica_plan = draw_replica_plan(jax.random.fold_in(key_list[9], 71), 0)
    capacity = draw_capacity(jax.random.fold_in(key_list[9], 71), 0)
    return dict(tokens_in=tokens_in, route_ids=route_ids, route_gates=route_gates, cotangent=cotangent, gate_proj=gate_proj, up_proj=up_proj, down_proj=down_proj, replica_plan=replica_plan, capacity=capacity)


def unpair(weights):
    count = weights.shape[0]
    spread = weights.reshape(count, D // 2, N_DP, 2, FF // N_DP)
    return spread.transpose(0, 1, 3, 2, 4).reshape(count, D, FF)


def pair(weights):
    count = weights.shape[0]
    spread = weights.reshape(count, D // 2, 2, N_DP, FF // N_DP)
    return spread.transpose(0, 1, 3, 2, 4).reshape(count, D // 2, 2 * FF)


def route_targets(batch_ids, batch_plan, batch_caps):
    expert_ids = jnp.arange(EXPERTS, dtype=jnp.int32)
    devices = jnp.arange(N_EXPERT, dtype=jnp.int32)
    hosting = (batch_plan[None, :] == expert_ids[:, None]).astype(jnp.int32)
    ranking = jnp.cumsum(hosting, axis=1)
    copies = 1 + ranking[:, -1]
    copy_ids = jnp.arange(N_EXPERT + 1, dtype=jnp.int32)
    matched = hosting[:, :, None] * (ranking[:, :, None] == copy_ids[None, None, :]).astype(jnp.int32)
    replica_dev = jnp.sum(matched * devices[None, :, None], axis=1)
    home_target = 3 * (expert_ids // 2) + expert_ids % 2
    target_table = jnp.where(copy_ids[None, :] == 0, home_target[:, None], 3 * replica_dev + 2).astype(jnp.int32)
    ids_dev = batch_ids.reshape(N_EXPERT, TOK_DEV * TOPK).astype(jnp.int32)
    token_of = (jnp.arange(TOKENS * TOPK, dtype=jnp.int32) // TOPK).reshape(N_EXPERT, TOK_DEV * TOPK)
    chosen = (token_of % copies[ids_dev]).astype(jnp.int32)
    target = target_table[ids_dev, chosen]
    limits = batch_caps[ids_dev]
    slot_ids = jnp.arange(3 * N_EXPERT, dtype=jnp.int32)
    onehot = (target[:, :, None] == slot_ids[None, None, :]).astype(jnp.int32)
    before = jnp.sum((jnp.cumsum(onehot, axis=1) - onehot) * onehot, axis=2)
    return target, before, before < limits


def expert_pass(rows_x, rows_grad, gate_w, up_w, down_w):
    quarter = FF // N_DP
    pre_gate = jnp.dot(rows_x, gate_w, preferred_element_type=jnp.float32)
    pre_up = jnp.dot(rows_x, up_w, preferred_element_type=jnp.float32)
    logistic = jax.nn.sigmoid(pre_gate)
    swished = pre_gate * logistic
    hidden = (swished * pre_up).astype(jnp.bfloat16)
    hidden_parts = hidden.astype(jnp.float32).reshape(-1, N_DP, quarter)
    down_parts = down_w.astype(jnp.float32).reshape(N_DP, quarter, D)
    partial_value = lax.optimization_barrier(jnp.einsum("rqf,qfd->qrd", hidden_parts, down_parts).astype(jnp.bfloat16))
    out_route = jnp.sum(partial_value.astype(jnp.float32), axis=0).astype(jnp.bfloat16)
    hidden_grad = jnp.dot(rows_grad, down_w.T, preferred_element_type=jnp.float32)
    gate_pre_grad = (hidden_grad * pre_up * logistic * (1.0 + pre_gate * (1.0 - logistic))).astype(jnp.bfloat16)
    up_pre_grad = (hidden_grad * swished).astype(jnp.bfloat16)
    gate_parts = gate_w.astype(jnp.float32).reshape(D, N_DP, quarter)
    up_parts = up_w.astype(jnp.float32).reshape(D, N_DP, quarter)
    gate_terms = jnp.einsum("rqf,dqf->qrd", gate_pre_grad.astype(jnp.float32).reshape(-1, N_DP, quarter), gate_parts)
    up_terms = jnp.einsum("rqf,dqf->qrd", up_pre_grad.astype(jnp.float32).reshape(-1, N_DP, quarter), up_parts)
    input_partial = lax.optimization_barrier((gate_terms + up_terms).astype(jnp.bfloat16))
    in_route = jnp.sum(input_partial.astype(jnp.float32), axis=0).astype(jnp.bfloat16)
    grads = (jnp.dot(rows_x.T, gate_pre_grad, preferred_element_type=jnp.float32),
             jnp.dot(rows_x.T, up_pre_grad, preferred_element_type=jnp.float32),
             jnp.dot(hidden.T, rows_grad, preferred_element_type=jnp.float32))
    return out_route, in_route, grads


def reference(tokens_in, route_ids, route_gates, cotangent, gate_proj, up_proj, down_proj, replica_plan, capacity):
    gate_full = unpair(gate_proj)
    up_full = unpair(up_proj)
    down_full = unpair(down_proj).transpose(0, 2, 1)
    sentinel = MICRO * TOKENS * TOPK
    devices = jnp.arange(N_EXPERT, dtype=jnp.int32)
    route_table = jnp.full((MICRO, 3 * N_EXPERT, N_EXPERT, CAP), sentinel, dtype=jnp.int32)
    for batch_index in range(MICRO):
        target, before, kept_mask = route_targets(route_ids[batch_index], replica_plan[batch_index], capacity[batch_index])
        route_index = (batch_index * TOKENS * TOPK + jnp.arange(TOKENS * TOPK, dtype=jnp.int32)).reshape(N_EXPERT, TOK_DEV * TOPK)
        slot_index = jnp.where(kept_mask, target, 3 * N_EXPERT).astype(jnp.int32)
        source_index = jnp.broadcast_to(devices[:, None], target.shape).astype(jnp.int32)
        place_index = jnp.minimum(before, CAP - 1).astype(jnp.int32)
        route_table = route_table.at[batch_index, slot_index, source_index, place_index].set(route_index.astype(jnp.int32), mode="drop")
    x_rows = jnp.concatenate([tokens_in.reshape(MICRO * TOKENS, D), jnp.zeros((1, D), jnp.bfloat16)], axis=0)
    scaled = route_gates[:, :, :, None] * cotangent[:, :, None, :].astype(jnp.float32)
    grad_rows = jnp.concatenate([scaled.astype(jnp.bfloat16).reshape(sentinel, D), jnp.zeros((1, D), jnp.bfloat16)], axis=0)

    def run_slot(indices, expert):
        token_index = jnp.where(indices < sentinel, indices // TOPK, MICRO * TOKENS).astype(jnp.int32)
        return expert_pass(x_rows[token_index], grad_rows[indices], gate_full[expert], up_full[expert], down_full[expert])

    out_init = jnp.zeros((sentinel, D), jnp.bfloat16)

    def home_step(running, expert):
        out_routes, in_routes = running
        slot_number = (3 * (expert // 2) + expert % 2).astype(jnp.int32)
        indices = route_table[:, slot_number].reshape(-1)
        out_route, in_route, grads = run_slot(indices, expert)
        out_routes = out_routes.at[indices].set(out_route, mode="drop")
        in_routes = in_routes.at[indices].set(in_route, mode="drop")
        return (out_routes, in_routes), tuple(member.astype(jnp.bfloat16) for member in grads)

    (out_routes, in_routes), home_grads = lax.scan(home_step, (out_init, out_init), jnp.arange(EXPERTS, dtype=jnp.int32))
    totals_init = tuple(lax.optimization_barrier(member).astype(jnp.float32) for member in home_grads)

    def replica_step(running, instance):
        out_routes, in_routes, totals = running
        batch_index = (instance // N_EXPERT).astype(jnp.int32)
        device = (instance % N_EXPERT).astype(jnp.int32)
        expert = replica_plan[batch_index, device].astype(jnp.int32)
        indices = route_table[batch_index, 3 * device + 2].reshape(-1)
        out_route, in_route, grads = run_slot(indices, expert)
        out_routes = out_routes.at[indices].set(out_route, mode="drop")
        in_routes = in_routes.at[indices].set(in_route, mode="drop")
        totals = tuple(running_total.at[expert].add(lax.optimization_barrier(member.astype(jnp.bfloat16)).astype(jnp.float32))
                       for running_total, member in zip(totals, grads))
        return (out_routes, in_routes, totals), None

    (out_routes, in_routes, totals), unused = lax.scan(replica_step, (out_routes, in_routes, totals_init),
                                                      jnp.arange(MICRO * N_EXPERT, dtype=jnp.int32))
    gated = route_gates[:, :, :, None] * out_routes.reshape(MICRO, TOKENS, TOPK, D).astype(jnp.float32)
    y_out = jnp.sum(gated, axis=2).astype(jnp.bfloat16)
    x_grad = jnp.sum(in_routes.reshape(MICRO, TOKENS, TOPK, D).astype(jnp.float32), axis=2).astype(jnp.bfloat16)
    gate_out = pair(totals[0].astype(jnp.bfloat16))
    up_out = pair(totals[1].astype(jnp.bfloat16))
    down_out = pair(totals[2].astype(jnp.bfloat16).transpose(0, 2, 1))
    return (y_out, x_grad, gate_out, up_out, down_out)
```

```python
import functools

import jax
import jax.numpy as jnp
from jax import lax
from jax.experimental import pallas as pl
from jax.experimental.pallas import tpu as pltpu
from jax.sharding import PartitionSpec as P

GROUP = 16
BF = jnp.bfloat16
F32 = jnp.float32


def kept_routes(batch_ids, batch_plan, batch_caps, source, device_count):
    expert_count = batch_caps.shape[0]
    tok_count = batch_ids.shape[0]
    expert_ids = jnp.arange(expert_count, dtype=jnp.int32)
    hosting = (batch_plan[None, :] == expert_ids[:, None]).astype(jnp.int32)
    ranking = jnp.cumsum(hosting, axis=1)
    copies = 1 + ranking[:, -1]
    matches = (batch_ids[:, :, None] == expert_ids[None, None, :]).astype(jnp.int32)
    copies_route = jnp.sum(matches * copies[None, None, :], axis=2)
    limits = jnp.sum(matches * batch_caps[None, None, :], axis=2)
    token_ids = source * tok_count + jnp.arange(tok_count, dtype=jnp.int32)
    chosen = token_ids[:, None] % copies_route
    flat = (batch_ids * (device_count + 1) + chosen).reshape(-1)
    place = jnp.arange(flat.shape[0], dtype=jnp.int32)
    earlier = (flat[:, None] == flat[None, :]) & (place[None, :] < place[:, None])
    before = jnp.sum(earlier.astype(jnp.int32), axis=1).reshape(batch_ids.shape)
    return before < limits


def pairing(features, inverse):
    half = features // 2
    a = lax.broadcasted_iota(jnp.int32, (features, features), 0)
    b = lax.broadcasted_iota(jnp.int32, (features, features), 1)
    if inverse:
        a, b = b, a
    return (a == 2 * (b % half) + b // half).astype(F32).astype(BF)


def dot(a, b, dims=((1,), (0,))):
    return lax.dot_general(a, b, (dims, ((), ())), preferred_element_type=F32)


def stacked(w):
    half = w.shape[1] // 2
    return jnp.concatenate([w[:, :half], w[:, half:]], axis=0)


def pre_kernel(xc_ref, want_ref, wg_ref, wu_ref, wd_ref, out_ref, p_ref):
    experts = wg_ref.shape[0]
    features = 2 * wg_ref.shape[1]
    hidden = wg_ref.shape[2] // 2
    tokens = xc_ref.shape[0]
    top = want_ref.shape[0] // tokens
    perm = pairing(features, False)
    x = dot(xc_ref[:, :features], perm).astype(BF)
    c = dot(xc_ref[:, features:], perm).astype(BF)

    def expert(e, carry):
        for kind, (w_ref, rows) in enumerate(((wg_ref, x), (wu_ref, x), (wd_ref, c))):
            p_ref[kind, e] = dot(rows, stacked(w_ref[e])).astype(BF)
        return carry

    lax.fori_loop(0, experts, expert, 0)
    columns = lax.broadcasted_iota(jnp.int32, (GROUP * top, experts * GROUP), 1)

    def group(g, carry):
        first = pl.multiple_of(g * GROUP, GROUP)
        start = pl.multiple_of(g * (GROUP * top), GROUP * top)
        sel = (want_ref[pl.ds(start, GROUP * top), :] == columns).astype(F32).astype(BF)
        for kind in range(3):
            dense = p_ref[kind, :, pl.ds(first, GROUP), :].reshape(experts * GROUP, hidden)
            rows = dot(sel, dense).astype(BF)
            for pair in range(top // 2):
                lo = rows[2 * pair * GROUP : (2 * pair + 1) * GROUP]
                hi = rows[(2 * pair + 1) * GROUP : (2 * pair + 2) * GROUP]
                at = (kind * top + 2 * pair) * hidden
                out_ref[pl.ds(first, GROUP), at : at + 2 * hidden] = jnp.concatenate([lo, hi], axis=1)
        return carry

    lax.fori_loop(0, tokens // GROUP, group, 0)


def post_kernel(
    h_ref, xc_ref, want_ref, wg_ref, wu_ref, wd_ref, yx_ref, dg_ref, du_ref, dd_ref, hd_ref, acc_ref, y_ref
):
    experts = wg_ref.shape[0]
    pair_rows = wg_ref.shape[1]
    features = 2 * pair_rows
    hidden = wg_ref.shape[2] // 2
    tokens = xc_ref.shape[0]
    top = want_ref.shape[2] // GROUP
    step = pl.program_id(0)
    perm = pairing(features, False)
    back = pairing(features, True)
    x = dot(xc_ref[:, :features], perm).astype(BF)
    c = dot(xc_ref[:, features:], perm).astype(BF)
    slots = lax.broadcasted_iota(jnp.int32, (experts * GROUP, GROUP * top), 0)

    @pl.when(step == 0)
    def _():
        acc_ref[...] = jnp.zeros_like(acc_ref)

    y_ref[...] = jnp.zeros_like(y_ref)

    def group(g, carry):
        first = pl.multiple_of(g * GROUP, GROUP)
        sel = (slots == want_ref[g]).astype(F32).astype(BF)
        for kind in range(3):
            parts = []
            for pair in range(top // 2):
                at = (kind * top + 2 * pair) * hidden
                both = h_ref[pl.ds(first, GROUP), at : at + 2 * hidden]
                parts += [both[:, :hidden], both[:, hidden:]]
            dense = dot(sel, jnp.concatenate(parts, axis=0)).astype(BF)
            hd_ref[kind, :, pl.ds(first, GROUP), :] = dense.reshape(experts, GROUP, hidden)
        return carry

    lax.fori_loop(0, tokens // GROUP, group, 0)

    def expert(e, carry):
        value, gate_g, up_g = hd_ref[0, e], hd_ref[1, e], hd_ref[2, e]
        across = ((1,), (1,))
        y_ref[0] += dot(value, stacked(wd_ref[e]), across)
        y_ref[1] += dot(gate_g, stacked(wg_ref[e]), across) + dot(up_g, stacked(wu_ref[e]), across)
        down = ((0,), (0,))
        acc_ref[0, e] += dot(x, gate_g, down)
        acc_ref[1, e] += dot(x, up_g, down)
        acc_ref[2, e] += dot(c, value, down)
        return carry

    lax.fori_loop(0, experts, expert, 0)
    yx_ref[:, :features] = dot(y_ref[0].astype(BF), back).astype(BF)
    yx_ref[:, features:] = dot(y_ref[1].astype(BF), back).astype(BF)

    @pl.when(step == pl.num_programs(0) - 1)
    def _():
        def write(e, carry):
            for kind, d_ref in enumerate((dg_ref, du_ref, dd_ref)):
                total = acc_ref[kind, e].astype(BF)
                d_ref[e] = jnp.concatenate([total[:pair_rows], total[pair_rows:]], axis=1)
            return carry

        lax.fori_loop(0, experts, write, 0)


def whole(shape):
    return pl.BlockSpec(shape, lambda b: (0,) * len(shape))


def rows_of(shape):
    return pl.BlockSpec(shape, lambda b: (b,) + (0,) * (len(shape) - 1))


def params():
    return pltpu.CompilerParams(vmem_limit_bytes=58 * 2**20, dimension_semantics=("arbitrary",))


def shards(
    tokens_in, route_ids, route_gates, cotangent, gate_proj, up_proj, down_proj, replica_plan, capacity
):
    n = lax.axis_size("expert")
    source = lax.axis_index("expert")
    micro, tok, top = route_ids.shape
    experts, pair_rows, width = gate_proj.shape
    hidden = width // 2
    features = 2 * pair_rows
    local = micro * tok
    total = n * local
    block = min(total // 2, max(GROUP, 4096 // experts))
    blocks = total // block

    both = jnp.stack([tokens_in.reshape(local, -1), cotangent.reshape(local, -1)])
    full = lax.all_gather(both, "dp", axis=2, tiled=True)
    full = full.reshape(2, local, n, features).transpose(2, 1, 0, 3).reshape(n, local, 2 * features)
    xc = lax.all_to_all(full, "expert", split_axis=0, concat_axis=0, tiled=True)
    xc = xc.reshape(total, 2 * features)

    ids = lax.all_gather(route_ids.reshape(local, top), "expert", axis=0, tiled=True)
    want = ids.reshape(total // GROUP, GROUP, top) * GROUP
    want = want + jnp.arange(GROUP, dtype=jnp.int32)[None, :, None]
    want = want.transpose(0, 2, 1).reshape(total // GROUP, top * GROUP)

    weights = (gate_proj, up_proj, down_proj)
    partial_rows = pl.pallas_call(
        pre_kernel,
        grid=(blocks,),
        in_specs=[rows_of((block, 2 * features)), rows_of((block * top, 1))] + [whole(gate_proj.shape)] * 3,
        out_specs=rows_of((block, 3 * top * hidden)),
        out_shape=jax.ShapeDtypeStruct((total, 3 * top * hidden), BF),
        scratch_shapes=[pltpu.VMEM((3, experts, block, hidden), BF)],
        compiler_params=params(),
    )(xc, want.reshape(-1, 1), *weights)

    kept = jnp.stack(
        [kept_routes(route_ids[m], replica_plan[m], capacity[m], source, n) for m in range(micro)]
    ).reshape(local, top)
    spread = jnp.repeat(jnp.eye(top, dtype=F32), hidden, axis=1)
    kept_gate = jnp.where(kept, route_gates.reshape(local, top), 0.0)
    scale = jnp.dot(kept_gate, spread, precision=lax.Precision.HIGHEST)

    arrived = lax.all_to_all(
        partial_rows.reshape(n, local, -1), "expert", split_axis=0, concat_axis=0, tiled=True
    )
    sums = jnp.sum(arrived.astype(F32), axis=0)
    span = top * hidden
    pre_gate, pre_up, value = sums[:, :span], sums[:, span : 2 * span], sums[:, 2 * span :]
    logistic = jax.nn.sigmoid(pre_gate)
    swished = pre_gate * logistic
    value = value * scale
    mine = jnp.concatenate(
        [
            (swished * pre_up * scale).astype(BF),
            (value * pre_up * logistic * (1.0 + pre_gate * (1.0 - logistic))).astype(BF),
            (value * swished).astype(BF),
        ],
        axis=1,
    )
    everyone = lax.all_gather(mine, "expert", axis=0, tiled=True)

    yx, gate_grad, up_grad, down_grad = pl.pallas_call(
        post_kernel,
        grid=(blocks,),
        in_specs=[
            rows_of((block, 3 * span)),
            rows_of((block, 2 * features)),
            rows_of((block // GROUP, 1, top * GROUP)),
        ]
        + [whole(gate_proj.shape)] * 3,
        out_specs=[rows_of((block, 2 * features))] + [whole(gate_proj.shape)] * 3,
        out_shape=[jax.ShapeDtypeStruct((total, 2 * features), BF)]
        + [jax.ShapeDtypeStruct(gate_proj.shape, BF)] * 3,
        scratch_shapes=[
            pltpu.VMEM((3, experts, block, hidden), BF),
            pltpu.VMEM((3, experts, features, hidden), F32),
            pltpu.VMEM((2, block, features), F32),
        ],
        compiler_params=params(),
    )(everyone, xc, want.reshape(-1, 1, top * GROUP), *weights)

    home = lax.all_to_all(
        yx.reshape(n, local, 2 * features), "expert", split_axis=0, concat_axis=0, tiled=True
    )
    done = lax.psum_scatter(home, "dp", scatter_dimension=0, tiled=True)
    done = done.reshape(-1, local, 2, features).transpose(2, 1, 0, 3).reshape(2, micro, tok, -1)
    return done[0], done[1], gate_grad, up_grad, down_grad


def solution(mesh):
    split = P(None, "expert", "dp")
    tokens = P(None, "expert", None)
    in_specs = (split, tokens, tokens, split, split, split, split, P(), P())
    return jax.shard_map(shards, mesh=mesh, in_specs=in_specs, out_specs=(split,) * 5, check_vma=False)
```

```python
import functools

import jax
import jax.numpy as jnp
from jax import lax
from jax.experimental import pallas as pl
from jax.experimental.pallas import tpu as pltpu
from jax.sharding import PartitionSpec as P

GROUP = 16
BF = jnp.bfloat16
F32 = jnp.float32


def kept_routes(batch_ids, batch_plan, batch_caps, source, device_count):
    expert_count = batch_caps.shape[0]
    tok_count = batch_ids.shape[0]
    expert_ids = jnp.arange(expert_count, dtype=jnp.int32)
    hosting = (batch_plan[None, :] == expert_ids[:, None]).astype(jnp.int32)
    ranking = jnp.cumsum(hosting, axis=1)
    copies = 1 + ranking[:, -1]
    matches = (batch_ids[:, :, None] == expert_ids[None, None, :]).astype(jnp.int32)
    copies_route = jnp.sum(matches * copies[None, None, :], axis=2)
    limits = jnp.sum(matches * batch_caps[None, None, :], axis=2)
    token_ids = source * tok_count + jnp.arange(tok_count, dtype=jnp.int32)
    chosen = token_ids[:, None] % copies_route
    flat = (batch_ids * (device_count + 1) + chosen).reshape(-1)
    place = jnp.arange(flat.shape[0], dtype=jnp.int32)
    earlier = (flat[:, None] == flat[None, :]) & (place[None, :] < place[:, None])
    before = jnp.sum(earlier.astype(jnp.int32), axis=1).reshape(batch_ids.shape)
    return before < limits


def pairing(features, inverse):
    half = features // 2
    a = lax.broadcasted_iota(jnp.int32, (features, features), 0)
    b = lax.broadcasted_iota(jnp.int32, (features, features), 1)
    if inverse:
        a, b = b, a
    return (a == 2 * (b % half) + b // half).astype(F32).astype(BF)


def dot(a, b, dims=((1,), (0,))):
    return lax.dot_general(a, b, (dims, ((), ())), preferred_element_type=F32)


def stacked(w):
    half = w.shape[1] // 2
    return jnp.concatenate([w[:, :half], w[:, half:]], axis=0)


def pre_kernel(xc_ref, want_ref, wg_ref, wu_ref, wd_ref, out_ref, p_ref):
    experts = wg_ref.shape[0]
    features = 2 * wg_ref.shape[1]
    hidden = wg_ref.shape[2] // 2
    tokens = xc_ref.shape[0]
    top = want_ref.shape[2] // GROUP
    perm = pairing(features, False)
    x = dot(xc_ref[:, :features], perm).astype(BF)
    c = dot(xc_ref[:, features:], perm).astype(BF)

    def expert(e, carry):
        for kind, (w_ref, rows) in enumerate(((wg_ref, x), (wu_ref, x), (wd_ref, c))):
            p_ref[kind, e] = dot(rows, stacked(w_ref[e])).astype(BF)
        return carry

    lax.fori_loop(0, experts, expert, 0)
    slots = lax.broadcasted_iota(jnp.int32, (experts * GROUP, GROUP * top), 0)

    def group(g, carry):
        first = pl.multiple_of(g * GROUP, GROUP)
        sel = (slots == want_ref[g]).astype(F32).astype(BF)
        for kind in range(3):
            dense = p_ref[kind, :, pl.ds(first, GROUP), :].reshape(experts * GROUP, hidden)
            rows = dot(sel, dense, ((0,), (0,))).astype(BF)
            for pair in range(top // 2):
                lo = rows[2 * pair * GROUP : (2 * pair + 1) * GROUP]
                hi = rows[(2 * pair + 1) * GROUP : (2 * pair + 2) * GROUP]
                at = (kind * top + 2 * pair) * hidden
                out_ref[pl.ds(first, GROUP), at : at + 2 * hidden] = jnp.concatenate([lo, hi], axis=1)
        return carry

    lax.fori_loop(0, tokens // GROUP, group, 0)


def post_kernel(
    h_ref, xc_ref, want_ref, wg_ref, wu_ref, wd_ref, yx_ref, dg_ref, du_ref, dd_ref, hd_ref, acc_ref, y_ref
):
    experts = wg_ref.shape[0]
    pair_rows = wg_ref.shape[1]
    features = 2 * pair_rows
    hidden = wg_ref.shape[2] // 2
    tokens = xc_ref.shape[0]
    top = want_ref.shape[2] // GROUP
    step = pl.program_id(0)
    perm = pairing(features, False)
    back = pairing(features, True)
    x = dot(xc_ref[:, :features], perm).astype(BF)
    c = dot(xc_ref[:, features:], perm).astype(BF)
    slots = lax.broadcasted_iota(jnp.int32, (experts * GROUP, GROUP * top), 0)

    @pl.when(step == 0)
    def _():
        acc_ref[...] = jnp.zeros_like(acc_ref)

    y_ref[...] = jnp.zeros_like(y_ref)

    def group(g, carry):
        first = pl.multiple_of(g * GROUP, GROUP)
        sel = (slots == want_ref[g]).astype(F32).astype(BF)
        for kind in range(3):
            parts = []
            for pair in range(top // 2):
                at = (kind * top + 2 * pair) * hidden
                both = h_ref[pl.ds(first, GROUP), at : at + 2 * hidden]
                parts += [both[:, :hidden], both[:, hidden:]]
            dense = dot(sel, jnp.concatenate(parts, axis=0)).astype(BF)
            hd_ref[kind, :, pl.ds(first, GROUP), :] = dense.reshape(experts, GROUP, hidden)
        return carry

    lax.fori_loop(0, tokens // GROUP, group, 0)

    def expert(e, carry):
        value, gate_g, up_g = hd_ref[0, e], hd_ref[1, e], hd_ref[2, e]
        across = ((1,), (1,))
        y_ref[0] += dot(value, stacked(wd_ref[e]), across)
        y_ref[1] += dot(gate_g, stacked(wg_ref[e]), across) + dot(up_g, stacked(wu_ref[e]), across)
        down = ((0,), (0,))
        acc_ref[0, e] += dot(x, gate_g, down)
        acc_ref[1, e] += dot(x, up_g, down)
        acc_ref[2, e] += dot(c, value, down)
        return carry

    lax.fori_loop(0, experts, expert, 0)
    yx_ref[:, :features] = dot(y_ref[0].astype(BF), back).astype(BF)
    yx_ref[:, features:] = dot(y_ref[1].astype(BF), back).astype(BF)

    @pl.when(step == pl.num_programs(0) - 1)
    def _():
        def write(e, carry):
            for kind, d_ref in enumerate((dg_ref, du_ref, dd_ref)):
                total = acc_ref[kind, e].astype(BF)
                d_ref[e] = jnp.concatenate([total[:pair_rows], total[pair_rows:]], axis=1)
            return carry

        lax.fori_loop(0, experts, write, 0)


def remote(src, dst, send_sem, recv_sem, dp, expert):
    return pltpu.make_async_remote_copy(
        src_ref=src,
        dst_ref=dst,
        send_sem=send_sem,
        recv_sem=recv_sem,
        device_id=(dp, expert),
        device_id_type=pl.DeviceIdType.MESH,
    )


def greet(senders, count):
    barrier = pltpu.get_barrier_semaphore()
    for condition, dp, expert in senders:

        @pl.when(condition)
        def _():
            pl.semaphore_signal(
                barrier, inc=1, device_id=(dp, expert), device_id_type=pl.DeviceIdType.MESH
            )

    pl.semaphore_wait(barrier, count)


def scatter_kernel(n, dpn, send_ref, want_ref, out_ref, ids_ref, local_sem, send_sem, recv_sem):
    p, i = lax.axis_index("dp"), lax.axis_index("expert")
    share = n // dpn
    owner = i // share
    selfish = owner == p
    greet([((owner != p) | (k != i), owner, k) for k in range(n)], n - selfish.astype(jnp.int32))
    targets = [(q, share * p + s, s, q * share + s) for q in range(dpn) for s in range(share)]

    def copies(q, j, s, slot):
        return (
            remote(send_ref.at[s], out_ref.at[i], send_sem.at[0, slot], recv_sem.at[0, i], q, j),
            remote(want_ref, ids_ref.at[i], send_sem.at[1, slot], recv_sem.at[1, i], q, j),
        )

    def own():
        return (
            pltpu.make_async_copy(send_ref.at[i % share], out_ref.at[i], local_sem.at[0]),
            pltpu.make_async_copy(want_ref, ids_ref.at[i], local_sem.at[1]),
        )

    for q, j, s, slot in targets:

        @pl.when((q != p) | (j != i))
        def _():
            for copy in copies(q, j, s, slot):
                copy.start()

    @pl.when(selfish)
    def _():
        for copy in own():
            copy.start()

    for k in range(n):

        @pl.when((owner != p) | (k != i))
        def _():
            remote(send_ref.at[0], out_ref.at[k], send_sem.at[0, 0], recv_sem.at[0, k], owner, k).wait_recv()
            remote(want_ref, ids_ref.at[k], send_sem.at[1, 0], recv_sem.at[1, k], owner, k).wait_recv()

    for q, j, s, slot in targets:

        @pl.when((q != p) | (j != i))
        def _():
            for copy in copies(q, j, s, slot):
                copy.wait_send()

    @pl.when(selfish)
    def _():
        for copy in own():
            copy.wait()


def collect_kernel(n, dpn, yx_ref, out_ref, buf_ref, local_sem, send_sem, recv_sem):
    p, i = lax.axis_index("dp"), lax.axis_index("expert")
    share = n // dpn
    owner = i // share
    selfish = owner == p
    senders = [(q, share * p + s, q * share + s) for q in range(dpn) for s in range(share)]
    greet([((q != p) | (j != i), q, j) for q, j, slot in senders], n - selfish.astype(jnp.int32))
    mine = p * share + i % share

    def copy(k):
        return remote(yx_ref.at[k], buf_ref.at[mine], send_sem.at[k], recv_sem.at[mine], owner, k)

    for k in range(n):

        @pl.when((owner != p) | (k != i))
        def _():
            copy(k).start()

    @pl.when(selfish)
    def _():
        own = pltpu.make_async_copy(yx_ref.at[i], buf_ref.at[mine], local_sem)
        own.start()
        own.wait()

    for q, j, slot in senders:

        @pl.when((q != p) | (j != i))
        def _():
            remote(yx_ref.at[0], buf_ref.at[slot], send_sem.at[0], recv_sem.at[slot], q, j).wait_recv()

    features = yx_ref.shape[2] // 2
    for s in range(share):
        total = sum(buf_ref[q * share + s].astype(F32) for q in range(dpn)).astype(BF)
        for kind in range(2):
            out_ref[kind, :, s * features : (s + 1) * features] = total[:, kind * features : (kind + 1) * features]

    for k in range(n):

        @pl.when((owner != p) | (k != i))
        def _():
            copy(k).wait_send()


def gather_kernel(n, in_ref, out_ref, local_sem, send_sem, recv_sem):
    p, i = lax.axis_index("dp"), lax.axis_index("expert")
    line = n // 2
    a, b = i // 2, i % 2
    other = a * 2 + 1 - b
    always = a >= 0
    has_left, has_right = a > 0, a < line - 1
    greet(
        [(always, p, other), (has_left, p, i - 2), (has_right, p, i + 2)],
        1 + has_left.astype(jnp.int32) + has_right.astype(jnp.int32),
    )
    own = pltpu.make_async_copy(in_ref, out_ref.at[i], local_sem)
    own.start()
    started = []

    def send(condition, src, chunk, target):
        copy = remote(src, out_ref.at[chunk], send_sem.at[len(started)], recv_sem.at[chunk], p, target)
        started.append((condition, copy))
        pl.when(condition)(copy.start)

    def arrive(condition, chunk):
        copy = remote(in_ref, out_ref.at[chunk], send_sem.at[0], recv_sem.at[chunk], p, other)
        pl.when(condition)(copy.wait_recv)

    send(has_right, in_ref, i, i + 2)
    send(has_left, in_ref, i, i - 2)
    send(always, in_ref, i, other)
    for step in range(1, line):
        for sign in (-1, 1):
            from_there = (a >= step) if sign < 0 else (a + step < line)
            further = has_right if sign < 0 else has_left
            chunk = jnp.where(from_there, i + 2 * sign * step, i)
            arrive(from_there, chunk)
            send(from_there & further, out_ref.at[chunk], chunk, i - 2 * sign)
            send(from_there, out_ref.at[chunk], chunk, other)
    for k in range(line):
        arrive(always, 2 * k + 1 - b)
    for condition, copy in started:
        pl.when(condition)(copy.wait_send)
    own.wait()


def comm_params(number):
    return pltpu.CompilerParams(
        collective_id=number, has_side_effects=True, vmem_limit_bytes=58 * 2**20
    )


ANY = pl.BlockSpec(memory_space=pl.ANY)
DMA = pltpu.SemaphoreType.DMA


def whole(shape):
    return pl.BlockSpec(shape, lambda b: (0,) * len(shape))


def rows_of(shape):
    return pl.BlockSpec(shape, lambda b: (b,) + (0,) * (len(shape) - 1))


def params():
    return pltpu.CompilerParams(vmem_limit_bytes=58 * 2**20, dimension_semantics=("arbitrary",))


def shards(
    tokens_in, route_ids, route_gates, cotangent, gate_proj, up_proj, down_proj, replica_plan, capacity
):
    n = lax.axis_size("expert")
    source = lax.axis_index("expert")
    micro, tok, top = route_ids.shape
    experts, pair_rows, width = gate_proj.shape
    hidden = width // 2
    features = 2 * pair_rows
    local = micro * tok
    total = n * local
    block = min(total // 2, max(GROUP, 4096 // experts))
    blocks = total // block

    dpn = lax.axis_size("dp")
    direct = n <= 16 and n % dpn == 0 and n % 2 == 0

    want = route_ids.reshape(local // GROUP, GROUP, top) * GROUP
    want = want + jnp.arange(GROUP, dtype=jnp.int32)[None, :, None]
    want = want.transpose(0, 2, 1).reshape(local // GROUP, top * GROUP)
    if direct:
        share = n // dpn
        both = jnp.stack([tokens_in.reshape(local, share, -1), cotangent.reshape(local, share, -1)])
        both = both.transpose(2, 1, 0, 3).reshape(share, local, 2 * features)
        xc, want = pl.pallas_call(
            functools.partial(scatter_kernel, n, dpn),
            in_specs=[ANY, ANY],
            out_specs=[ANY, ANY],
            out_shape=[
                jax.ShapeDtypeStruct((n, local, 2 * features), BF),
                jax.ShapeDtypeStruct((n,) + want.shape, jnp.int32),
            ],
            scratch_shapes=[DMA((2,)), DMA((2, n)), DMA((2, n))],
            compiler_params=comm_params(0),
        )(both, want)
    else:
        both = jnp.stack([tokens_in.reshape(local, -1), cotangent.reshape(local, -1)])
        full = lax.all_gather(both, "dp", axis=2, tiled=True)
        full = full.reshape(2, local, n, features).transpose(2, 1, 0, 3).reshape(n, local, 2 * features)
        xc = lax.all_to_all(full, "expert", split_axis=0, concat_axis=0, tiled=True)
        want = lax.all_gather(want, "expert", axis=0, tiled=True)
    xc = xc.reshape(total, 2 * features)
    want = want.reshape(total // GROUP, 1, top * GROUP)

    weights = (gate_proj, up_proj, down_proj)
    partial_rows = pl.pallas_call(
        pre_kernel,
        grid=(blocks,),
        in_specs=[rows_of((block, 2 * features)), rows_of((block // GROUP, 1, top * GROUP))]
        + [whole(gate_proj.shape)] * 3,
        out_specs=rows_of((block, 3 * top * hidden)),
        out_shape=jax.ShapeDtypeStruct((total, 3 * top * hidden), BF),
        scratch_shapes=[pltpu.VMEM((3, experts, block, hidden), BF)],
        compiler_params=params(),
    )(xc, want, *weights)

    kept = jnp.stack(
        [kept_routes(route_ids[m], replica_plan[m], capacity[m], source, n) for m in range(micro)]
    ).reshape(local, top)
    spread = jnp.repeat(jnp.eye(top, dtype=F32), hidden, axis=1)
    kept_gate = jnp.where(kept, route_gates.reshape(local, top), 0.0)
    scale = jnp.dot(kept_gate, spread, precision=lax.Precision.HIGHEST)

    arrived = lax.all_to_all(
        partial_rows.reshape(n, local, -1), "expert", split_axis=0, concat_axis=0, tiled=True
    )
    sums = jnp.sum(arrived.astype(F32), axis=0)
    span = top * hidden
    pre_gate, pre_up, value = sums[:, :span], sums[:, span : 2 * span], sums[:, 2 * span :]
    logistic = jax.nn.sigmoid(pre_gate)
    swished = pre_gate * logistic
    value = value * scale
    mine = jnp.concatenate(
        [
            (swished * pre_up * scale).astype(BF),
            (value * pre_up * logistic * (1.0 + pre_gate * (1.0 - logistic))).astype(BF),
            (value * swished).astype(BF),
        ],
        axis=1,
    )
    if direct:
        everyone = pl.pallas_call(
            functools.partial(gather_kernel, n),
            in_specs=[ANY],
            out_specs=ANY,
            out_shape=jax.ShapeDtypeStruct((n, local, 3 * span), BF),
            scratch_shapes=[DMA, DMA((2 * n + 8,)), DMA((n,))],
            compiler_params=comm_params(1),
        )(mine).reshape(total, 3 * span)
    else:
        everyone = lax.all_gather(mine, "expert", axis=0, tiled=True)

    yx, gate_grad, up_grad, down_grad = pl.pallas_call(
        post_kernel,
        grid=(blocks,),
        in_specs=[
            rows_of((block, 3 * span)),
            rows_of((block, 2 * features)),
            rows_of((block // GROUP, 1, top * GROUP)),
        ]
        + [whole(gate_proj.shape)] * 3,
        out_specs=[rows_of((block, 2 * features))] + [whole(gate_proj.shape)] * 3,
        out_shape=[jax.ShapeDtypeStruct((total, 2 * features), BF)]
        + [jax.ShapeDtypeStruct(gate_proj.shape, BF)] * 3,
        scratch_shapes=[
            pltpu.VMEM((3, experts, block, hidden), BF),
            pltpu.VMEM((3, experts, features, hidden), F32),
            pltpu.VMEM((2, block, features), F32),
        ],
        compiler_params=params(),
    )(everyone, xc, want, *weights)

    yx = yx.reshape(n, local, 2 * features)
    if direct:
        done = pl.pallas_call(
            functools.partial(collect_kernel, n, dpn),
            in_specs=[ANY],
            out_specs=pl.BlockSpec(memory_space=pltpu.VMEM),
            out_shape=jax.ShapeDtypeStruct((2, local, n // dpn * features), BF),
            scratch_shapes=[pltpu.VMEM((n, local, 2 * features), BF), DMA, DMA((n,)), DMA((n,))],
            compiler_params=comm_params(2),
        )(yx)
    else:
        home = lax.all_to_all(yx, "expert", split_axis=0, concat_axis=0, tiled=True)
        done = lax.psum_scatter(home, "dp", scatter_dimension=0, tiled=True)
        done = done.reshape(-1, local, 2, features).transpose(2, 1, 0, 3)
    done = done.reshape(2, micro, tok, -1)
    return done[0], done[1], gate_grad, up_grad, down_grad


def solution(mesh):
    split = P(None, "expert", "dp")
    tokens = P(None, "expert", None)
    in_specs = (split, tokens, tokens, split, split, split, split, P(), P())
    return jax.shard_map(shards, mesh=mesh, in_specs=in_specs, out_specs=(split,) * 5, check_vma=False)
```

```python
import functools

import jax
import jax.numpy as jnp
from jax import lax
from jax.experimental import pallas as pl
from jax.experimental.pallas import tpu as pltpu
from jax.sharding import PartitionSpec as P

GROUP = 16
BF = jnp.bfloat16
F32 = jnp.float32


def kept_routes(batch_ids, batch_plan, batch_caps, source, device_count):
    expert_count = batch_caps.shape[0]
    tok_count = batch_ids.shape[0]
    expert_ids = jnp.arange(expert_count, dtype=jnp.int32)
    hosting = (batch_plan[None, :] == expert_ids[:, None]).astype(jnp.int32)
    ranking = jnp.cumsum(hosting, axis=1)
    copies = 1 + ranking[:, -1]
    matches = (batch_ids[:, :, None] == expert_ids[None, None, :]).astype(jnp.int32)
    copies_route = jnp.sum(matches * copies[None, None, :], axis=2)
    limits = jnp.sum(matches * batch_caps[None, None, :], axis=2)
    token_ids = source * tok_count + jnp.arange(tok_count, dtype=jnp.int32)
    chosen = token_ids[:, None] % copies_route
    flat = (batch_ids * (device_count + 1) + chosen).reshape(-1)
    place = jnp.arange(flat.shape[0], dtype=jnp.int32)
    earlier = (flat[:, None] == flat[None, :]) & (place[None, :] < place[:, None])
    before = jnp.sum(earlier.astype(jnp.int32), axis=1).reshape(batch_ids.shape)
    return before < limits


def pairing(features, inverse):
    half = features // 2
    a = lax.broadcasted_iota(jnp.int32, (features, features), 0)
    b = lax.broadcasted_iota(jnp.int32, (features, features), 1)
    if inverse:
        a, b = b, a
    return (a == 2 * (b % half) + b // half).astype(F32).astype(BF)


def dot(a, b, dims=((1,), (0,))):
    return lax.dot_general(a, b, (dims, ((), ())), preferred_element_type=F32)


def stacked(w):
    half = w.shape[1] // 2
    return jnp.concatenate([w[:, :half], w[:, half:]], axis=0)


def pre_kernel(xc_ref, want_ref, wg_ref, wu_ref, wd_ref, out_ref, p_ref):
    experts = wg_ref.shape[0]
    features = 2 * wg_ref.shape[1]
    hidden = wg_ref.shape[2] // 2
    tokens = xc_ref.shape[0]
    top = want_ref.shape[2] // GROUP
    perm = pairing(features, False)
    x = dot(xc_ref[:, :features], perm).astype(BF)
    c = dot(xc_ref[:, features:], perm).astype(BF)

    def expert(e, carry):
        for kind, (w_ref, rows) in enumerate(((wg_ref, x), (wu_ref, x), (wd_ref, c))):
            p_ref[kind, e] = dot(rows, stacked(w_ref[e])).astype(BF)
        return carry

    lax.fori_loop(0, experts, expert, 0)
    slots = lax.broadcasted_iota(jnp.int32, (experts * GROUP, GROUP * top), 0)

    def group(g, carry):
        first = pl.multiple_of(g * GROUP, GROUP)
        sel = (slots == want_ref[g]).astype(F32).astype(BF)
        for kind in range(3):
            dense = p_ref[kind, :, pl.ds(first, GROUP), :].reshape(experts * GROUP, hidden)
            rows = dot(sel, dense, ((0,), (0,))).astype(BF)
            for pair in range(top // 2):
                lo = rows[2 * pair * GROUP : (2 * pair + 1) * GROUP]
                hi = rows[(2 * pair + 1) * GROUP : (2 * pair + 2) * GROUP]
                at = (kind * top + 2 * pair) * hidden
                out_ref[pl.ds(first, GROUP), at : at + 2 * hidden] = jnp.concatenate([lo, hi], axis=1)
        return carry

    lax.fori_loop(0, tokens // GROUP, group, 0)


def post_kernel(
    h_ref, xc_ref, want_ref, wg_ref, wu_ref, wd_ref, yx_ref, dg_ref, du_ref, dd_ref, hd_ref, acc_ref, y_ref
):
    experts = wg_ref.shape[0]
    pair_rows = wg_ref.shape[1]
    features = 2 * pair_rows
    hidden = wg_ref.shape[2] // 2
    tokens = xc_ref.shape[0]
    top = want_ref.shape[2] // GROUP
    step = pl.program_id(0)
    perm = pairing(features, False)
    back = pairing(features, True)
    x = dot(perm, xc_ref[:, :features], ((0,), (1,))).astype(BF)
    c = dot(perm, xc_ref[:, features:], ((0,), (1,))).astype(BF)
    slots = lax.broadcasted_iota(jnp.int32, (experts * GROUP, GROUP * top), 0)

    @pl.when(step == 0)
    def _():
        acc_ref[...] = jnp.zeros_like(acc_ref)

    y_ref[...] = jnp.zeros_like(y_ref)

    def group(g, carry):
        first = pl.multiple_of(g * GROUP, GROUP)
        sel = (slots == want_ref[g]).astype(F32).astype(BF)
        for kind in range(3):
            parts = []
            for pair in range(top // 2):
                at = (kind * top + 2 * pair) * hidden
                both = h_ref[pl.ds(first, GROUP), at : at + 2 * hidden]
                parts += [both[:, :hidden], both[:, hidden:]]
            dense = dot(sel, jnp.concatenate(parts, axis=0)).astype(BF)
            hd_ref[kind, :, pl.ds(first, GROUP), :] = dense.reshape(experts, GROUP, hidden)
        return carry

    lax.fori_loop(0, tokens // GROUP, group, 0)

    def expert(e, carry):
        value, gate_g, up_g = hd_ref[0, e], hd_ref[1, e], hd_ref[2, e]
        across = ((1,), (1,))
        y_ref[0] += dot(value, stacked(wd_ref[e]), across)
        y_ref[1] += dot(gate_g, stacked(wg_ref[e]), across) + dot(up_g, stacked(wu_ref[e]), across)
        acc_ref[0, e] += dot(x, gate_g)
        acc_ref[1, e] += dot(x, up_g)
        acc_ref[2, e] += dot(c, value)
        return carry

    lax.fori_loop(0, experts, expert, 0)
    yx_ref[:, :features] = dot(y_ref[0].astype(BF), back).astype(BF)
    yx_ref[:, features:] = dot(y_ref[1].astype(BF), back).astype(BF)

    @pl.when(step == pl.num_programs(0) - 1)
    def _():
        def write(e, carry):
            for kind, d_ref in enumerate((dg_ref, du_ref, dd_ref)):
                total = acc_ref[kind, e].astype(BF)
                d_ref[e] = jnp.concatenate([total[:pair_rows], total[pair_rows:]], axis=1)
            return carry

        lax.fori_loop(0, experts, write, 0)


def remote(src, dst, send_sem, recv_sem, dp, expert):
    return pltpu.make_async_remote_copy(
        src_ref=src,
        dst_ref=dst,
        send_sem=send_sem,
        recv_sem=recv_sem,
        device_id=(dp, expert),
        device_id_type=pl.DeviceIdType.MESH,
    )


def greet(senders, count):
    barrier = pltpu.get_barrier_semaphore()
    for condition, dp, expert in senders:

        @pl.when(condition)
        def _():
            pl.semaphore_signal(
                barrier, inc=1, device_id=(dp, expert), device_id_type=pl.DeviceIdType.MESH
            )

    pl.semaphore_wait(barrier, count)


def scatter_kernel(n, dpn, send_ref, want_ref, out_ref, ids_ref, local_sem, send_sem, recv_sem):
    p, i = lax.axis_index("dp"), lax.axis_index("expert")
    share = n // dpn
    owner = i // share
    selfish = owner == p
    greet([((owner != p) | (k != i), owner, k) for k in range(n)], n - selfish.astype(jnp.int32))
    targets = [(q, share * p + s, s, q * share + s) for q in range(dpn) for s in range(share)]

    def copies(q, j, s, slot):
        return (
            remote(send_ref.at[s], out_ref.at[i], send_sem.at[0, slot], recv_sem.at[0, i], q, j),
            remote(want_ref, ids_ref.at[i], send_sem.at[1, slot], recv_sem.at[1, i], q, j),
        )

    def own():
        return (
            pltpu.make_async_copy(send_ref.at[i % share], out_ref.at[i], local_sem.at[0]),
            pltpu.make_async_copy(want_ref, ids_ref.at[i], local_sem.at[1]),
        )

    for q, j, s, slot in targets:

        @pl.when((q != p) | (j != i))
        def _():
            for copy in copies(q, j, s, slot):
                copy.start()

    @pl.when(selfish)
    def _():
        for copy in own():
            copy.start()

    for k in range(n):

        @pl.when((owner != p) | (k != i))
        def _():
            remote(send_ref.at[0], out_ref.at[k], send_sem.at[0, 0], recv_sem.at[0, k], owner, k).wait_recv()
            remote(want_ref, ids_ref.at[k], send_sem.at[1, 0], recv_sem.at[1, k], owner, k).wait_recv()

    for q, j, s, slot in targets:

        @pl.when((q != p) | (j != i))
        def _():
            for copy in copies(q, j, s, slot):
                copy.wait_send()

    @pl.when(selfish)
    def _():
        for copy in own():
            copy.wait()


def collect_kernel(n, dpn, yx_ref, out_ref, buf_ref, local_sem, send_sem, recv_sem):
    p, i = lax.axis_index("dp"), lax.axis_index("expert")
    share = n // dpn
    owner = i // share
    selfish = owner == p
    senders = [(q, share * p + s, q * share + s) for q in range(dpn) for s in range(share)]
    greet([((q != p) | (j != i), q, j) for q, j, slot in senders], n - selfish.astype(jnp.int32))
    mine = p * share + i % share

    def copy(k):
        return remote(yx_ref.at[k], buf_ref.at[mine], send_sem.at[k], recv_sem.at[mine], owner, k)

    for k in range(n):

        @pl.when((owner != p) | (k != i))
        def _():
            copy(k).start()

    @pl.when(selfish)
    def _():
        own = pltpu.make_async_copy(yx_ref.at[i], buf_ref.at[mine], local_sem)
        own.start()
        own.wait()

    for q, j, slot in senders:

        @pl.when((q != p) | (j != i))
        def _():
            remote(yx_ref.at[0], buf_ref.at[slot], send_sem.at[0], recv_sem.at[slot], q, j).wait_recv()

    features = yx_ref.shape[2] // 2
    for s in range(share):
        total = sum(buf_ref[q * share + s].astype(F32) for q in range(dpn)).astype(BF)
        for kind in range(2):
            out_ref[kind, :, s * features : (s + 1) * features] = total[:, kind * features : (kind + 1) * features]

    for k in range(n):

        @pl.when((owner != p) | (k != i))
        def _():
            copy(k).wait_send()


def activate(pre_gate, pre_up, value, scale):
    logistic = jax.nn.sigmoid(pre_gate)
    swished = pre_gate * logistic
    value = value * scale
    return (
        (swished * pre_up * scale).astype(BF),
        (value * pre_up * logistic * (1.0 + pre_gate * (1.0 - logistic))).astype(BF),
        (value * swished).astype(BF),
    )


def reduce_kernel(
    n, pieces, in_ref, scale_ref, out_ref, y_ref, stage_ref, z_ref, sum_ref, y_send, y_recv, z_send, z_recv
):
    p, i = lax.axis_index("dp"), lax.axis_index("expert")
    line = n // 2
    a, b = i // 2, i % 2
    other = a * 2 + 1 - b
    always = a >= 0
    has_left, has_right = a > 0, a < line - 1
    rows = in_ref.shape[1] // pieces
    span = scale_ref.shape[1]
    greet(
        [(always, p, other), (has_left, p, i - 2), (has_right, p, i + 2)],
        1 + has_left.astype(jnp.int32) + has_right.astype(jnp.int32),
    )
    order = []
    for k in range((line + 1) // 2):
        order += [line - 1 - k] if line - 1 - k == k else [line - 1 - k, k]

    def across(h, d):
        at = pl.ds(h * rows, rows)
        return remote(
            in_ref.at[2 * d + 1 - b, at], y_ref.at[d, at], y_send.at[h, d], y_recv.at[h, d], p, other
        )

    def along(h, d, side):
        at = pl.ds(h * rows, rows)
        target = i + 2 if side == 0 else i - 2
        return remote(
            stage_ref.at[d, at], z_ref.at[side, d, at], z_send.at[h, d], z_recv.at[side, h, d], p, target
        )

    def add(target, terms):
        def body(k, carry):
            at = pl.ds(pl.multiple_of(k * span, span), span)
            total = terms[0][:, at].astype(F32)
            for term in terms[1:]:
                total = total + term[:, at].astype(F32)
            target[:, at] = total.astype(target.dtype)
            return carry

        lax.fori_loop(0, 3, body, 0)

    for h in range(pieces):
        for d in order:
            across(h, d).start()

    for h in range(pieces):
        at = pl.ds(h * rows, rows)
        for d in order:
            across(h, d).wait_recv()
            both = [in_ref.at[2 * d + b, at], y_ref.at[d, at]]
            for side in range(2):
                passing = a < d if side == 0 else a > d
                behind = has_left if side == 0 else has_right

                @pl.when(passing)
                def _():
                    @pl.when(behind)
                    def _():
                        along(h, d, side).wait_recv()
                        add(stage_ref.at[d, at], both + [z_ref.at[side, d, at]])

                    @pl.when(jnp.logical_not(behind))
                    def _():
                        add(stage_ref.at[d, at], both)

                    along(h, d, side).start()

    for h in range(pieces):
        at = pl.ds(h * rows, rows)
        total = sum_ref.at[at]
        add(total, [in_ref.at[i, at], y_ref.at[a, at]])
        for side in range(2):

            @pl.when(has_left if side == 0 else has_right)
            def _():
                along(h, a, side).wait_recv()
                add(total, [total, z_ref.at[side, a, at]])

        parts = activate(
            sum_ref[at, :span], sum_ref[at, span : 2 * span], sum_ref[at, 2 * span :], scale_ref[at, :]
        )
        for kind, part in enumerate(parts):
            out_ref[at, kind * span : (kind + 1) * span] = part

    for h in range(pieces):
        for d in order:
            across(h, d).wait_send()
            for side in range(2):
                pl.when(a < d if side == 0 else a > d)(along(h, d, side).wait_send)


def gather_kernel(n, in_ref, out_ref, local_sem, send_sem, recv_sem):
    p, i = lax.axis_index("dp"), lax.axis_index("expert")
    line = n // 2
    a, b = i // 2, i % 2
    other = a * 2 + 1 - b
    always = a >= 0
    has_left, has_right = a > 0, a < line - 1
    greet(
        [(always, p, other), (has_left, p, i - 2), (has_right, p, i + 2)],
        1 + has_left.astype(jnp.int32) + has_right.astype(jnp.int32),
    )
    own = pltpu.make_async_copy(in_ref, out_ref.at[i], local_sem)
    own.start()
    started = []

    def send(condition, src, chunk, target):
        copy = remote(src, out_ref.at[chunk], send_sem.at[len(started)], recv_sem.at[chunk], p, target)
        started.append((condition, copy))
        pl.when(condition)(copy.start)

    def arrive(condition, chunk):
        copy = remote(in_ref, out_ref.at[chunk], send_sem.at[0], recv_sem.at[chunk], p, other)
        pl.when(condition)(copy.wait_recv)

    send(has_right, in_ref, i, i + 2)
    send(has_left, in_ref, i, i - 2)
    send(always, in_ref, i, other)
    for step in range(1, line):
        for sign in (-1, 1):
            from_there = (a >= step) if sign < 0 else (a + step < line)
            further = has_right if sign < 0 else has_left
            chunk = jnp.where(from_there, i + 2 * sign * step, i)
            arrive(from_there, chunk)
            send(from_there & further, out_ref.at[chunk], chunk, i - 2 * sign)
            send(from_there, out_ref.at[chunk], chunk, other)
    for k in range(line):
        arrive(always, 2 * k + 1 - b)
    for condition, copy in started:
        pl.when(condition)(copy.wait_send)
    own.wait()


def comm_params(number):
    return pltpu.CompilerParams(
        collective_id=number, has_side_effects=True, vmem_limit_bytes=58 * 2**20
    )


ANY = pl.BlockSpec(memory_space=pl.ANY)
DMA = pltpu.SemaphoreType.DMA


def whole(shape):
    return pl.BlockSpec(shape, lambda b: (0,) * len(shape))


def rows_of(shape):
    return pl.BlockSpec(shape, lambda b: (b,) + (0,) * (len(shape) - 1))


def params():
    return pltpu.CompilerParams(vmem_limit_bytes=58 * 2**20, dimension_semantics=("arbitrary",))


def shards(
    tokens_in, route_ids, route_gates, cotangent, gate_proj, up_proj, down_proj, replica_plan, capacity
):
    n = lax.axis_size("expert")
    source = lax.axis_index("expert")
    micro, tok, top = route_ids.shape
    experts, pair_rows, width = gate_proj.shape
    hidden = width // 2
    features = 2 * pair_rows
    local = micro * tok
    total = n * local
    block = min(total // 2, max(GROUP, 4096 // experts))
    blocks = total // block

    dpn = lax.axis_size("dp")
    direct = n <= 16 and n % dpn == 0 and n % 2 == 0

    want = route_ids.reshape(local // GROUP, GROUP, top) * GROUP
    want = want + jnp.arange(GROUP, dtype=jnp.int32)[None, :, None]
    want = want.transpose(0, 2, 1).reshape(local // GROUP, top * GROUP)
    if direct:
        share = n // dpn
        both = jnp.stack([tokens_in.reshape(local, share, -1), cotangent.reshape(local, share, -1)])
        both = both.transpose(2, 1, 0, 3).reshape(share, local, 2 * features)
        xc, want = pl.pallas_call(
            functools.partial(scatter_kernel, n, dpn),
            in_specs=[ANY, ANY],
            out_specs=[ANY, ANY],
            out_shape=[
                jax.ShapeDtypeStruct((n, local, 2 * features), BF),
                jax.ShapeDtypeStruct((n,) + want.shape, jnp.int32),
            ],
            scratch_shapes=[DMA((2,)), DMA((2, n)), DMA((2, n))],
            compiler_params=comm_params(0),
        )(both, want)
    else:
        both = jnp.stack([tokens_in.reshape(local, -1), cotangent.reshape(local, -1)])
        full = lax.all_gather(both, "dp", axis=2, tiled=True)
        full = full.reshape(2, local, n, features).transpose(2, 1, 0, 3).reshape(n, local, 2 * features)
        xc = lax.all_to_all(full, "expert", split_axis=0, concat_axis=0, tiled=True)
        want = lax.all_gather(want, "expert", axis=0, tiled=True)
    xc = xc.reshape(total, 2 * features)
    want = want.reshape(total // GROUP, 1, top * GROUP)

    weights = (gate_proj, up_proj, down_proj)
    partial_rows = pl.pallas_call(
        pre_kernel,
        grid=(blocks,),
        in_specs=[rows_of((block, 2 * features)), rows_of((block // GROUP, 1, top * GROUP))]
        + [whole(gate_proj.shape)] * 3,
        out_specs=rows_of((block, 3 * top * hidden)),
        out_shape=jax.ShapeDtypeStruct((total, 3 * top * hidden), BF),
        scratch_shapes=[pltpu.VMEM((3, experts, block, hidden), BF)],
        compiler_params=params(),
    )(xc, want, *weights)

    kept = jnp.stack(
        [kept_routes(route_ids[m], replica_plan[m], capacity[m], source, n) for m in range(micro)]
    ).reshape(local, top)
    spread = jnp.repeat(jnp.eye(top, dtype=F32), hidden, axis=1)
    kept_gate = jnp.where(kept, route_gates.reshape(local, top), 0.0)
    scale = jnp.dot(kept_gate, spread, precision=lax.Precision.HIGHEST)

    span = top * hidden
    partial_rows = partial_rows.reshape(n, local, 3 * span)
    if direct:
        pieces = 2 if local % 32 == 0 else 1
        slots = (n // 2, local, 3 * span)
        vmem = pl.BlockSpec(memory_space=pltpu.VMEM)
        mine = pl.pallas_call(
            functools.partial(reduce_kernel, n, pieces),
            in_specs=[vmem, vmem],
            out_specs=vmem,
            out_shape=jax.ShapeDtypeStruct((local, 3 * span), BF),
            scratch_shapes=[
                pltpu.VMEM(slots, BF),
                pltpu.VMEM(slots, BF),
                pltpu.VMEM((2,) + slots, BF),
                pltpu.VMEM((local, 3 * span), F32),
                DMA((pieces, n // 2)),
                DMA((pieces, n // 2)),
                DMA((pieces, n // 2)),
                DMA((2, pieces, n // 2)),
            ],
            compiler_params=comm_params(3),
        )(partial_rows, scale)
    else:
        arrived = lax.all_to_all(partial_rows, "expert", split_axis=0, concat_axis=0, tiled=True)
        sums = jnp.sum(arrived.astype(F32), axis=0)
        parts = activate(sums[:, :span], sums[:, span : 2 * span], sums[:, 2 * span :], scale)
        mine = jnp.concatenate(parts, axis=1)
    if direct:
        everyone = pl.pallas_call(
            functools.partial(gather_kernel, n),
            in_specs=[ANY],
            out_specs=ANY,
            out_shape=jax.ShapeDtypeStruct((n, local, 3 * span), BF),
            scratch_shapes=[DMA, DMA((2 * n + 8,)), DMA((n,))],
            compiler_params=comm_params(1),
        )(mine).reshape(total, 3 * span)
    else:
        everyone = lax.all_gather(mine, "expert", axis=0, tiled=True)

    yx, gate_grad, up_grad, down_grad = pl.pallas_call(
        post_kernel,
        grid=(blocks,),
        in_specs=[
            rows_of((block, 3 * span)),
            rows_of((block, 2 * features)),
            rows_of((block // GROUP, 1, top * GROUP)),
        ]
        + [whole(gate_proj.shape)] * 3,
        out_specs=[rows_of((block, 2 * features))] + [whole(gate_proj.shape)] * 3,
        out_shape=[jax.ShapeDtypeStruct((total, 2 * features), BF)]
        + [jax.ShapeDtypeStruct(gate_proj.shape, BF)] * 3,
        scratch_shapes=[
            pltpu.VMEM((3, experts, block, hidden), BF),
            pltpu.VMEM((3, experts, features, hidden), F32),
            pltpu.VMEM((2, block, features), F32),
        ],
        compiler_params=params(),
    )(everyone, xc, want, *weights)

    yx = yx.reshape(n, local, 2 * features)
    if direct:
        done = pl.pallas_call(
            functools.partial(collect_kernel, n, dpn),
            in_specs=[ANY],
            out_specs=pl.BlockSpec(memory_space=pltpu.VMEM),
            out_shape=jax.ShapeDtypeStruct((2, local, n // dpn * features), BF),
            scratch_shapes=[pltpu.VMEM((n, local, 2 * features), BF), DMA, DMA((n,)), DMA((n,))],
            compiler_params=comm_params(2),
        )(yx)
    else:
        home = lax.all_to_all(yx, "expert", split_axis=0, concat_axis=0, tiled=True)
        done = lax.psum_scatter(home, "dp", scatter_dimension=0, tiled=True)
        done = done.reshape(-1, local, 2, features).transpose(2, 1, 0, 3)
    done = done.reshape(2, micro, tok, -1)
    return done[0], done[1], gate_grad, up_grad, down_grad


def solution(mesh):
    split = P(None, "expert", "dp")
    tokens = P(None, "expert", None)
    in_specs = (split, tokens, tokens, split, split, split, split, P(), P())
    return jax.shard_map(shards, mesh=mesh, in_specs=in_specs, out_specs=(split,) * 5, check_vma=False)
```

```python
import functools

import jax
import jax.numpy as jnp
from jax import lax
from jax.experimental import pallas as pl
from jax.experimental.pallas import tpu as pltpu
from jax.sharding import PartitionSpec as P

GROUP = 16
BF = jnp.bfloat16
F32 = jnp.float32


def kept_routes(batch_ids, batch_plan, batch_caps, source, device_count):
    expert_count = batch_caps.shape[0]
    tok_count = batch_ids.shape[0]
    expert_ids = jnp.arange(expert_count, dtype=jnp.int32)
    hosting = (batch_plan[None, :] == expert_ids[:, None]).astype(jnp.int32)
    ranking = jnp.cumsum(hosting, axis=1)
    copies = 1 + ranking[:, -1]
    matches = (batch_ids[:, :, None] == expert_ids[None, None, :]).astype(jnp.int32)
    copies_route = jnp.sum(matches * copies[None, None, :], axis=2)
    limits = jnp.sum(matches * batch_caps[None, None, :], axis=2)
    token_ids = source * tok_count + jnp.arange(tok_count, dtype=jnp.int32)
    chosen = token_ids[:, None] % copies_route
    flat = (batch_ids * (device_count + 1) + chosen).reshape(-1)
    place = jnp.arange(flat.shape[0], dtype=jnp.int32)
    earlier = (flat[:, None] == flat[None, :]) & (place[None, :] < place[:, None])
    before = jnp.sum(earlier.astype(jnp.int32), axis=1).reshape(batch_ids.shape)
    return before < limits


def pairing(features, inverse):
    half = features // 2
    a = lax.broadcasted_iota(jnp.int32, (features, features), 0)
    b = lax.broadcasted_iota(jnp.int32, (features, features), 1)
    if inverse:
        a, b = b, a
    return (a == 2 * (b % half) + b // half).astype(F32).astype(BF)


def dot(a, b, dims=((1,), (0,))):
    return lax.dot_general(a, b, (dims, ((), ())), preferred_element_type=F32)


def stacked(w):
    half = w.shape[1] // 2
    return jnp.concatenate([w[:, :half], w[:, half:]], axis=0)


def pre_kernel(xc_ref, want_ref, wg_ref, wu_ref, wd_ref, out_ref, p_ref):
    experts = wg_ref.shape[0]
    features = 2 * wg_ref.shape[1]
    hidden = wg_ref.shape[2] // 2
    tokens = xc_ref.shape[0]
    top = want_ref.shape[2] // GROUP
    perm = pairing(features, False)
    x = dot(xc_ref[:, :features], perm).astype(BF)
    c = dot(xc_ref[:, features:], perm).astype(BF)

    def expert(e, carry):
        for kind, (w_ref, rows) in enumerate(((wg_ref, x), (wu_ref, x), (wd_ref, c))):
            p_ref[kind, e] = dot(rows, stacked(w_ref[e])).astype(BF)
        return carry

    lax.fori_loop(0, experts, expert, 0, unroll=4)
    slots = lax.broadcasted_iota(jnp.int32, (experts * GROUP, GROUP * top), 0)

    def group(g, carry):
        first = pl.multiple_of(g * GROUP, GROUP)
        sel = (slots == want_ref[g]).astype(F32).astype(BF)
        for kind in range(3):
            dense = p_ref[kind, :, pl.ds(first, GROUP), :].reshape(experts * GROUP, hidden)
            rows = dot(sel, dense, ((0,), (0,))).astype(BF)
            for pair in range(top // 2):
                lo = rows[2 * pair * GROUP : (2 * pair + 1) * GROUP]
                hi = rows[(2 * pair + 1) * GROUP : (2 * pair + 2) * GROUP]
                at = (kind * top + 2 * pair) * hidden
                out_ref[pl.ds(first, GROUP), at : at + 2 * hidden] = jnp.concatenate([lo, hi], axis=1)
        return carry

    lax.fori_loop(0, tokens // GROUP, group, 0, unroll=2)


def post_kernel(
    h_ref, xc_ref, want_ref, wg_ref, wu_ref, wd_ref, yx_ref, dg_ref, du_ref, dd_ref, hd_ref, acc_ref, y_ref
):
    experts = wg_ref.shape[0]
    pair_rows = wg_ref.shape[1]
    features = 2 * pair_rows
    hidden = wg_ref.shape[2] // 2
    tokens = xc_ref.shape[0]
    top = want_ref.shape[2] // GROUP
    step = pl.program_id(0)
    perm = pairing(features, False)
    back = pairing(features, True)
    x = dot(perm, xc_ref[:, :features], ((0,), (1,))).astype(BF)
    c = dot(perm, xc_ref[:, features:], ((0,), (1,))).astype(BF)
    slots = lax.broadcasted_iota(jnp.int32, (experts * GROUP, GROUP * top), 0)

    @pl.when(step == 0)
    def _():
        acc_ref[...] = jnp.zeros_like(acc_ref)

    y_ref[...] = jnp.zeros_like(y_ref)

    def group(g, carry):
        first = pl.multiple_of(g * GROUP, GROUP)
        sel = (slots == want_ref[g]).astype(F32).astype(BF)
        for kind in range(3):
            parts = []
            for pair in range(top // 2):
                at = (kind * top + 2 * pair) * hidden
                both = h_ref[pl.ds(first, GROUP), at : at + 2 * hidden]
                parts += [both[:, :hidden], both[:, hidden:]]
            dense = dot(sel, jnp.concatenate(parts, axis=0)).astype(BF)
            hd_ref[kind, :, pl.ds(first, GROUP), :] = dense.reshape(experts, GROUP, hidden)
        return carry

    lax.fori_loop(0, tokens // GROUP, group, 0, unroll=2)

    def expert(e, carry):
        value, gate_g, up_g = hd_ref[0, e], hd_ref[1, e], hd_ref[2, e]
        across = ((1,), (1,))
        y_ref[0] += dot(value, stacked(wd_ref[e]), across)
        y_ref[1] += dot(gate_g, stacked(wg_ref[e]), across) + dot(up_g, stacked(wu_ref[e]), across)
        acc_ref[0, e] += dot(x, gate_g)
        acc_ref[1, e] += dot(x, up_g)
        acc_ref[2, e] += dot(c, value)
        return carry

    lax.fori_loop(0, experts, expert, 0, unroll=4)
    yx_ref[:, :features] = dot(y_ref[0].astype(BF), back).astype(BF)
    yx_ref[:, features:] = dot(y_ref[1].astype(BF), back).astype(BF)

    @pl.when(step == pl.num_programs(0) - 1)
    def _():
        def write(e, carry):
            for kind, d_ref in enumerate((dg_ref, du_ref, dd_ref)):
                total = acc_ref[kind, e].astype(BF)
                d_ref[e] = jnp.concatenate([total[:pair_rows], total[pair_rows:]], axis=1)
            return carry

        lax.fori_loop(0, experts, write, 0)


def remote(src, dst, send_sem, recv_sem, dp, expert):
    return pltpu.make_async_remote_copy(
        src_ref=src,
        dst_ref=dst,
        send_sem=send_sem,
        recv_sem=recv_sem,
        device_id=(dp, expert),
        device_id_type=pl.DeviceIdType.MESH,
    )


def greet(senders, count):
    barrier = pltpu.get_barrier_semaphore()
    for condition, dp, expert in senders:

        @pl.when(condition)
        def _():
            pl.semaphore_signal(
                barrier, inc=1, device_id=(dp, expert), device_id_type=pl.DeviceIdType.MESH
            )

    pl.semaphore_wait(barrier, count)


def scatter_kernel(n, dpn, send_ref, want_ref, out_ref, ids_ref, local_sem, send_sem, recv_sem):
    p, i = lax.axis_index("dp"), lax.axis_index("expert")
    share = n // dpn
    owner = i // share
    selfish = owner == p
    greet([((owner != p) | (k != i), owner, k) for k in range(n)], n - selfish.astype(jnp.int32))
    targets = [(q, share * p + s, s, q * share + s) for q in range(dpn) for s in range(share)]

    def copies(q, j, s, slot):
        return (
            remote(send_ref.at[s], out_ref.at[i], send_sem.at[0, slot], recv_sem.at[0, i], q, j),
            remote(want_ref, ids_ref.at[i], send_sem.at[1, slot], recv_sem.at[1, i], q, j),
        )

    def own():
        return (
            pltpu.make_async_copy(send_ref.at[i % share], out_ref.at[i], local_sem.at[0]),
            pltpu.make_async_copy(want_ref, ids_ref.at[i], local_sem.at[1]),
        )

    for q, j, s, slot in targets:

        @pl.when((q != p) | (j != i))
        def _():
            for copy in copies(q, j, s, slot):
                copy.start()

    @pl.when(selfish)
    def _():
        for copy in own():
            copy.start()

    for k in range(n):

        @pl.when((owner != p) | (k != i))
        def _():
            remote(send_ref.at[0], out_ref.at[k], send_sem.at[0, 0], recv_sem.at[0, k], owner, k).wait_recv()
            remote(want_ref, ids_ref.at[k], send_sem.at[1, 0], recv_sem.at[1, k], owner, k).wait_recv()

    for q, j, s, slot in targets:

        @pl.when((q != p) | (j != i))
        def _():
            for copy in copies(q, j, s, slot):
                copy.wait_send()

    @pl.when(selfish)
    def _():
        for copy in own():
            copy.wait()


def collect_kernel(n, dpn, yx_ref, out_ref, buf_ref, local_sem, send_sem, recv_sem):
    p, i = lax.axis_index("dp"), lax.axis_index("expert")
    share = n // dpn
    owner = i // share
    selfish = owner == p
    senders = [(q, share * p + s, q * share + s) for q in range(dpn) for s in range(share)]
    greet([((q != p) | (j != i), q, j) for q, j, slot in senders], n - selfish.astype(jnp.int32))
    mine = p * share + i % share

    def copy(k):
        return remote(yx_ref.at[k], buf_ref.at[mine], send_sem.at[k], recv_sem.at[mine], owner, k)

    for k in range(n):

        @pl.when((owner != p) | (k != i))
        def _():
            copy(k).start()

    @pl.when(selfish)
    def _():
        own = pltpu.make_async_copy(yx_ref.at[i], buf_ref.at[mine], local_sem)
        own.start()
        own.wait()

    for q, j, slot in senders:

        @pl.when((q != p) | (j != i))
        def _():
            remote(yx_ref.at[0], buf_ref.at[slot], send_sem.at[0], recv_sem.at[slot], q, j).wait_recv()

    features = yx_ref.shape[2] // 2
    for s in range(share):
        total = sum(buf_ref[q * share + s].astype(F32) for q in range(dpn)).astype(BF)
        for kind in range(2):
            out_ref[kind, :, s * features : (s + 1) * features] = total[:, kind * features : (kind + 1) * features]

    for k in range(n):

        @pl.when((owner != p) | (k != i))
        def _():
            copy(k).wait_send()


def activate(pre_gate, pre_up, value, scale):
    logistic = jax.nn.sigmoid(pre_gate)
    swished = pre_gate * logistic
    value = value * scale
    return (
        (swished * pre_up * scale).astype(BF),
        (value * pre_up * logistic * (1.0 + pre_gate * (1.0 - logistic))).astype(BF),
        (value * swished).astype(BF),
    )


def reduce_kernel(
    n, pieces, in_ref, scale_ref, out_ref, y_ref, stage_ref, z_ref, sum_ref, y_send, y_recv, z_send, z_recv
):
    p, i = lax.axis_index("dp"), lax.axis_index("expert")
    line = n // 2
    a, b = i // 2, i % 2
    other = a * 2 + 1 - b
    always = a >= 0
    has_left, has_right = a > 0, a < line - 1
    rows = in_ref.shape[1] // pieces
    span = scale_ref.shape[1]
    greet(
        [(always, p, other), (has_left, p, i - 2), (has_right, p, i + 2)],
        1 + has_left.astype(jnp.int32) + has_right.astype(jnp.int32),
    )
    order = []
    for k in range((line + 1) // 2):
        order += [line - 1 - k] if line - 1 - k == k else [line - 1 - k, k]

    def across(h, d):
        at = pl.ds(h * rows, rows)
        return remote(
            in_ref.at[2 * d + 1 - b, at], y_ref.at[d, at], y_send.at[h, d], y_recv.at[h, d], p, other
        )

    def along(h, d, side):
        at = pl.ds(h * rows, rows)
        target = i + 2 if side == 0 else i - 2
        return remote(
            stage_ref.at[d, at], z_ref.at[side, d, at], z_send.at[h, d], z_recv.at[side, h, d], p, target
        )

    def add(target, terms):
        def body(k, carry):
            at = pl.ds(pl.multiple_of(k * span, span), span)
            total = terms[0][:, at].astype(F32)
            for term in terms[1:]:
                total = total + term[:, at].astype(F32)
            target[:, at] = total.astype(target.dtype)
            return carry

        lax.fori_loop(0, 3, body, 0)

    for h in range(pieces):
        for d in order:
            across(h, d).start()

    for h in range(pieces):
        at = pl.ds(h * rows, rows)
        for d in order:
            across(h, d).wait_recv()
            both = [in_ref.at[2 * d + b, at], y_ref.at[d, at]]
            for side in range(2):
                passing = a < d if side == 0 else a > d
                behind = has_left if side == 0 else has_right

                @pl.when(passing)
                def _():
                    @pl.when(behind)
                    def _():
                        along(h, d, side).wait_recv()
                        add(stage_ref.at[d, at], both + [z_ref.at[side, d, at]])

                    @pl.when(jnp.logical_not(behind))
                    def _():
                        add(stage_ref.at[d, at], both)

                    along(h, d, side).start()

    for h in range(pieces):
        at = pl.ds(h * rows, rows)
        total = sum_ref.at[at]
        add(total, [in_ref.at[i, at], y_ref.at[a, at]])
        for side in range(2):

            @pl.when(has_left if side == 0 else has_right)
            def _():
                along(h, a, side).wait_recv()
                add(total, [total, z_ref.at[side, a, at]])

        parts = activate(
            sum_ref[at, :span], sum_ref[at, span : 2 * span], sum_ref[at, 2 * span :], scale_ref[at, :]
        )
        for kind, part in enumerate(parts):
            out_ref[at, kind * span : (kind + 1) * span] = part

    for h in range(pieces):
        for d in order:
            across(h, d).wait_send()
            for side in range(2):
                pl.when(a < d if side == 0 else a > d)(along(h, d, side).wait_send)


def gather_kernel(n, pieces, in_ref, out_ref, local_sem, send_sem, recv_sem):
    p, i = lax.axis_index("dp"), lax.axis_index("expert")
    line = n // 2
    a, b = i // 2, i % 2
    other = a * 2 + 1 - b
    always = a >= 0
    has_left, has_right = a > 0, a < line - 1
    rows = in_ref.shape[0] // pieces
    greet(
        [(always, p, other), (has_left, p, i - 2), (has_right, p, i + 2)],
        1 + has_left.astype(jnp.int32) + has_right.astype(jnp.int32),
    )
    started = []

    def send(condition, own, h, chunk, target):
        at = pl.ds(h * rows, rows)
        src = in_ref.at[at] if own else out_ref.at[chunk, at]
        copy = remote(
            src, out_ref.at[chunk, at], send_sem.at[len(started)], recv_sem.at[h, chunk], p, target
        )
        started.append((condition, copy))
        pl.when(condition)(copy.start)

    def arrive(condition, h, chunk):
        at = pl.ds(h * rows, rows)
        copy = remote(in_ref.at[at], out_ref.at[chunk, at], send_sem.at[0], recv_sem.at[h, chunk], p, other)
        pl.when(condition)(copy.wait_recv)

    for h in range(pieces):
        send(has_right, True, h, i, i + 2)
        send(has_left, True, h, i, i - 2)
        send(always, True, h, i, other)
    own = pltpu.make_async_copy(in_ref, out_ref.at[i], local_sem)
    own.start()
    for step in range(1, line):
        for h in range(pieces):
            for sign in (-1, 1):
                from_there = (a >= step) if sign < 0 else (a + step < line)
                further = has_right if sign < 0 else has_left
                chunk = jnp.where(from_there, i + 2 * sign * step, i)
                arrive(from_there, h, chunk)
                send(from_there & further, False, h, chunk, i - 2 * sign)
                send(from_there, False, h, chunk, other)
    for k in range(line):
        for h in range(pieces):
            arrive(always, h, 2 * k + 1 - b)
    for condition, copy in started:
        pl.when(condition)(copy.wait_send)
    own.wait()


def comm_params(number):
    return pltpu.CompilerParams(
        collective_id=number, has_side_effects=True, vmem_limit_bytes=58 * 2**20
    )


ANY = pl.BlockSpec(memory_space=pl.ANY)
DMA = pltpu.SemaphoreType.DMA


def whole(shape):
    return pl.BlockSpec(shape, lambda b: (0,) * len(shape))


def rows_of(shape):
    return pl.BlockSpec(shape, lambda b: (b,) + (0,) * (len(shape) - 1))


def params():
    return pltpu.CompilerParams(vmem_limit_bytes=58 * 2**20, dimension_semantics=("arbitrary",))


def shards(
    tokens_in, route_ids, route_gates, cotangent, gate_proj, up_proj, down_proj, replica_plan, capacity
):
    n = lax.axis_size("expert")
    source = lax.axis_index("expert")
    micro, tok, top = route_ids.shape
    experts, pair_rows, width = gate_proj.shape
    hidden = width // 2
    features = 2 * pair_rows
    local = micro * tok
    total = n * local
    block = min(total // 2, max(GROUP, 4096 // experts))
    blocks = total // block

    dpn = lax.axis_size("dp")
    direct = n <= 16 and n % dpn == 0 and n % 2 == 0

    want = route_ids.reshape(local // GROUP, GROUP, top) * GROUP
    want = want + jnp.arange(GROUP, dtype=jnp.int32)[None, :, None]
    want = want.transpose(0, 2, 1).reshape(local // GROUP, top * GROUP)
    if direct:
        share = n // dpn
        both = jnp.stack([tokens_in.reshape(local, share, -1), cotangent.reshape(local, share, -1)])
        both = both.transpose(2, 1, 0, 3).reshape(share, local, 2 * features)
        xc, want = pl.pallas_call(
            functools.partial(scatter_kernel, n, dpn),
            in_specs=[ANY, ANY],
            out_specs=[ANY, ANY],
            out_shape=[
                jax.ShapeDtypeStruct((n, local, 2 * features), BF),
                jax.ShapeDtypeStruct((n,) + want.shape, jnp.int32),
            ],
            scratch_shapes=[DMA((2,)), DMA((2, n)), DMA((2, n))],
            compiler_params=comm_params(0),
        )(both, want)
    else:
        both = jnp.stack([tokens_in.reshape(local, -1), cotangent.reshape(local, -1)])
        full = lax.all_gather(both, "dp", axis=2, tiled=True)
        full = full.reshape(2, local, n, features).transpose(2, 1, 0, 3).reshape(n, local, 2 * features)
        xc = lax.all_to_all(full, "expert", split_axis=0, concat_axis=0, tiled=True)
        want = lax.all_gather(want, "expert", axis=0, tiled=True)
    xc = xc.reshape(total, 2 * features)
    want = want.reshape(total // GROUP, 1, top * GROUP)

    weights = (gate_proj, up_proj, down_proj)
    partial_rows = pl.pallas_call(
        pre_kernel,
        grid=(blocks,),
        in_specs=[rows_of((block, 2 * features)), rows_of((block // GROUP, 1, top * GROUP))]
        + [whole(gate_proj.shape)] * 3,
        out_specs=rows_of((block, 3 * top * hidden)),
        out_shape=jax.ShapeDtypeStruct((total, 3 * top * hidden), BF),
        scratch_shapes=[pltpu.VMEM((3, experts, block, hidden), BF)],
        compiler_params=params(),
    )(xc, want, *weights)

    kept = jnp.stack(
        [kept_routes(route_ids[m], replica_plan[m], capacity[m], source, n) for m in range(micro)]
    ).reshape(local, top)
    spread = jnp.repeat(jnp.eye(top, dtype=F32), hidden, axis=1)
    kept_gate = jnp.where(kept, route_gates.reshape(local, top), 0.0)
    scale = jnp.dot(kept_gate, spread, precision=lax.Precision.HIGHEST)

    span = top * hidden
    partial_rows = partial_rows.reshape(n, local, 3 * span)
    if direct:
        pieces = 4 if local % 64 == 0 else 1
        slots = (n // 2, local, 3 * span)
        vmem = pl.BlockSpec(memory_space=pltpu.VMEM)
        mine = pl.pallas_call(
            functools.partial(reduce_kernel, n, pieces),
            in_specs=[vmem, vmem],
            out_specs=vmem,
            out_shape=jax.ShapeDtypeStruct((local, 3 * span), BF),
            scratch_shapes=[
                pltpu.VMEM(slots, BF),
                pltpu.VMEM(slots, BF),
                pltpu.VMEM((2,) + slots, BF),
                pltpu.VMEM((local, 3 * span), F32),
                DMA((pieces, n // 2)),
                DMA((pieces, n // 2)),
                DMA((pieces, n // 2)),
                DMA((2, pieces, n // 2)),
            ],
            compiler_params=comm_params(3),
        )(partial_rows, scale)
    else:
        arrived = lax.all_to_all(partial_rows, "expert", split_axis=0, concat_axis=0, tiled=True)
        sums = jnp.sum(arrived.astype(F32), axis=0)
        parts = activate(sums[:, :span], sums[:, span : 2 * span], sums[:, 2 * span :], scale)
        mine = jnp.concatenate(parts, axis=1)
    if direct:
        everyone = pl.pallas_call(
            functools.partial(gather_kernel, n, 2 if local % 32 == 0 else 1),
            in_specs=[ANY],
            out_specs=ANY,
            out_shape=jax.ShapeDtypeStruct((n, local, 3 * span), BF),
            scratch_shapes=[DMA, DMA((4 * n + 8,)), DMA((2, n))],
            compiler_params=comm_params(1),
        )(mine).reshape(total, 3 * span)
    else:
        everyone = lax.all_gather(mine, "expert", axis=0, tiled=True)

    yx, gate_grad, up_grad, down_grad = pl.pallas_call(
        post_kernel,
        grid=(blocks,),
        in_specs=[
            rows_of((block, 3 * span)),
            rows_of((block, 2 * features)),
            rows_of((block // GROUP, 1, top * GROUP)),
        ]
        + [whole(gate_proj.shape)] * 3,
        out_specs=[rows_of((block, 2 * features))] + [whole(gate_proj.shape)] * 3,
        out_shape=[jax.ShapeDtypeStruct((total, 2 * features), BF)]
        + [jax.ShapeDtypeStruct(gate_proj.shape, BF)] * 3,
        scratch_shapes=[
            pltpu.VMEM((3, experts, block, hidden), BF),
            pltpu.VMEM((3, experts, features, hidden), F32),
            pltpu.VMEM((2, block, features), F32),
        ],
        compiler_params=params(),
    )(everyone, xc, want, *weights)

    yx = yx.reshape(n, local, 2 * features)
    if direct:
        done = pl.pallas_call(
            functools.partial(collect_kernel, n, dpn),
            in_specs=[ANY],
            out_specs=pl.BlockSpec(memory_space=pltpu.VMEM),
            out_shape=jax.ShapeDtypeStruct((2, local, n // dpn * features), BF),
            scratch_shapes=[pltpu.VMEM((n, local, 2 * features), BF), DMA, DMA((n,)), DMA((n,))],
            compiler_params=comm_params(2),
        )(yx)
    else:
        home = lax.all_to_all(yx, "expert", split_axis=0, concat_axis=0, tiled=True)
        done = lax.psum_scatter(home, "dp", scatter_dimension=0, tiled=True)
        done = done.reshape(-1, local, 2, features).transpose(2, 1, 0, 3)
    done = done.reshape(2, micro, tok, -1)
    return done[0], done[1], gate_grad, up_grad, down_grad


def solution(mesh):
    split = P(None, "expert", "dp")
    tokens = P(None, "expert", None)
    in_specs = (split, tokens, tokens, split, split, split, split, P(), P())
    return jax.shard_map(shards, mesh=mesh, in_specs=in_specs, out_specs=(split,) * 5, check_vma=False)
```
